32 devices in a mesh: group: 2 (over x), wx: 16 (over z, y, core).
Axes of the slice: x: 2, y: 2, z: 4, core: 2. Of those that a mesh axis runs over, the one named last changes fastest.
Arguments:
- hidden_in: bfloat16 [8, 16384], P('group', 'wx'), parts along dimension 0, may hold values from -4000 to 4000
- norm_gain: bfloat16 [16384], P('wx'), may hold values from 0.099609375 to 1.8984375
- w_query: bfloat16 [16384, 8192], P('wx'), may hold values from -0.0625 to 0.0625
- w_key: bfloat16 [16384, 512], P('wx'), may hold values from -0.0625 to 0.0625
- w_value: bfloat16 [16384, 512], P('wx'), may hold values from -0.0625 to 0.0625
- w_out: bfloat16 [8192, 16384], P('wx'), may hold values from -0.1875 to 0.1875
- key_cache: bfloat16 [32, 8192, 128], P(('group', 'wx')), parts along dimension 0, may hold values from -800 to 800
- value_cache: bfloat16 [32, 8192, 128], P(('group', 'wx')), parts along dimension 0, may hold values from -6 to 6
- lengths: int32 [8], P('group'), parts along dimension 0, may hold values from 16 to 8192, as said below
Outputs:
- block_out: bfloat16 [8, 16384], P('group', 'wx'), parts along dimension 0
The draws below stay inside these ranges and needn't reach their ends.
There are 2 independent parts, one for each index of `group`. The reference program is written for one: setup_inputs(seed, part) draws one part's arguments, and reference() takes and returns one part's arrays. A program takes and returns all parts, laid end to end along the dimension named above; an argument that names none is the same for every part. Nothing has to cross between parts.
Inputs may be any that keep to these rules, and one draw needn't show every extreme that they name: `lengths`: some row holds exactly 8192 cached tokens and some row exactly 16.
All inputs are finite; a program needn't handle non-finite values.
Results may differ from the reference program's by a relative error of at most 0.012.
The reference program's roundings to bfloat16 on the way (of `scaled`, `query`, `probs` and `attended`) count: a program that leaves them out, or rounds other values in their place, can miss the bound.
Values may be sent and summed in bfloat16 or wider, within the bound.
A program may use at most 128 MiB of HBM per device.

```python
import jax
import jax.numpy as jnp
from jax import lax

D = 16384
HD = 128
KVH = 4
G = 16
CTX = 8192
QH = 64
SLOTS = 16
BATCH = 4


def draw_hidden_in(key, part):
    key = jax.random.fold_in(key, 11)
    key_base, key_cols, key_rows = jax.random.split(key, 3)
    columns = jnp.arange(D, dtype=jnp.float32) / D
    col_scale = jnp.exp(jax.random.uniform(key_cols, (D,), jnp.float32) * jnp.log(10.0))
    row_scale = jnp.exp(jax.random.uniform(key_rows, (BATCH, 1), jnp.float32) * jnp.log(10.0))
    base = jax.random.truncated_normal(key_base, -4.0, 4.0, (BATCH, D), jnp.float32)
    ramp = jnp.exp(jnp.log(3.0) * columns)
    return (base * col_scale[None, :] * ramp[None, :] * row_scale).astype(jnp.bfloat16)


def draw_key_cache(key, part):
    key = jax.random.fold_in(key, 23)
    key_base = jax.random.fold_in(key, 0)
    return jax.random.truncated_normal(key_base, -4.0, 4.0, (SLOTS, CTX, HD), jnp.float32).astype(jnp.bfloat16)


def draw_lengths(key, part):
    key = jax.random.fold_in(key, 37)
    key_vals, key_short, key_flag, key_pick, key_other = jax.random.split(key, 5)
    values = jax.random.randint(key_vals, (BATCH,), 16, CTX + 1, dtype=jnp.int32)
    short = jax.random.randint(key_short, (BATCH,), 16, min(48, CTX) + 1, dtype=jnp.int32)
    flags = jax.random.randint(key_flag, (BATCH,), 0, 8, dtype=jnp.int32) == 0
    values = jnp.where(flags, short, values)
    chosen = jax.random.randint(key_pick, (), 0, BATCH, dtype=jnp.int32)
    other = (chosen + 1 + jax.random.randint(key_other, (), 0, BATCH - 1, dtype=jnp.int32)) % BATCH
    rows = jnp.arange(BATCH, dtype=jnp.int32)
    values = jnp.where(rows == other, 16, values)
    return jnp.where(rows == chosen, CTX, values).astype(jnp.int32)


def with_spikes(values, rng, source, target, parts, factor):
    owner, partner = [(jnp.arange(values.shape[position]) // (values.shape[position] // parts)).reshape([-1 if axis == position else 1 for axis in range(values.ndim)]) for position in (source, target)]
    chosen = jax.random.permutation(rng, parts)[partner]
    strong = (owner == chosen) | (owner == (partner + parts // 2) % parts)
    return jnp.where(strong, factor * values, values)


def levels(rng, dims, cuts, smallest, top_value):
    loudness, own = 1.0, jax.random.fold_in(rng, 6)
    for axis_at, blocks in cuts:
        draws = jnp.exp(jax.random.uniform(jax.random.fold_in(own, axis_at), (blocks,), jnp.float32, smallest / len(cuts), top_value / len(cuts)))
        loudness = loudness * jnp.repeat(draws, dims[axis_at] // blocks).reshape([-1 if axis == axis_at else 1 for axis in range(len(dims))])
    return loudness


def bell_draw(key, extent, scale, most, cuts=(), held_as=jnp.bfloat16):
    level = levels(key, extent, cuts, -0.22, 0.18) if cuts else 1.0
    drawn = jax.random.normal(key, extent, jnp.float32) * scale * level
    return jnp.minimum(jnp.maximum(drawn, -most), most).astype(held_as)


def bell_draw_with(stream_key, extent, scale, limit, cuts, heavy, kind=jnp.bfloat16):
    values = scale * jax.random.normal(stream_key, extent, jnp.float32)
    if cuts:
        values = values * levels(stream_key, extent, cuts, -0.22, 0.18)
    return jnp.clip(with_spikes(values, jax.random.fold_in(stream_key, 3), *heavy), -limit, limit).astype(kind)


def setup_inputs(seed: int = 0, part: int = 0) -> dict:
    seeds = jax.random.split(jax.random.key(seed), 10)
    part_keys = jax.random.split(jax.random.fold_in(seeds[9], part), 10)
    hidden_in = draw_hidden_in(jax.random.fold_in(jax.random.fold_in(seeds[9], part), 71), part)
    norm_gain = jnp.clip(1.0 + 0.18 * jax.random.normal(seeds[1], (D,), jnp.float32), 0.099609375, 1.8984375).astype(jnp.bfloat16)
    w_query = bell_draw_with(seeds[2], (D, QH * HD), D ** -0.5, 0.0625, ((0, 16),), (0, 1, 16, 2.0))
    w_key = bell_draw_with(seeds[3], (D, KVH * HD), D ** -0.5, 0.0625, ((0, 16),), (0, 1, 16, 2.0))
    w_value = bell_draw_with(seeds[4], (D, KVH * HD), D ** -0.5, 0.0625, ((0, 16),), (0, 1, 16, 2.0))
    w_out = bell_draw_with(seeds[5], (QH * HD, D), (G * HD) ** -0.5, 0.1875, ((0, 16),), (0, 1, 16, 2.0))
    key_cache = draw_key_cache(jax.random.fold_in(jax.random.fold_in(seeds[9], part), 71), part)
    value_cache = bell_draw(part_keys[7], (SLOTS, CTX, HD), 1.0, 6.0, ((0, 16),))
    lengths = draw_lengths(jax.random.fold_in(jax.random.fold_in(seeds[9], part), 71), part)
    return {"hidden_in": hidden_in, "norm_gain": norm_gain, "w_query": w_query, "w_key": w_key, "w_value": w_value, "w_out": w_out, "key_cache": key_cache, "value_cache": value_cache, "lengths": lengths}


def attend_slot(query_heads, key_block, value_block, fresh_key, fresh_value, length):
    factor = HD ** (-0.5)
    scores = jnp.dot(query_heads, key_block.T, preferred_element_type=jnp.float32) * factor
    positions = jnp.arange(CTX, dtype=jnp.int32)
    scores = jnp.where(positions[None, :] < length, scores, -jnp.inf)
    own_score = jnp.dot(query_heads, fresh_key, preferred_element_type=jnp.float32) * factor
    highest = jnp.maximum(lax.optimization_barrier(jnp.max(scores, axis=1)), own_score)
    weights = jnp.exp(scores - highest[:, None])
    own_weight = jnp.exp(own_score - highest)
    total = lax.optimization_barrier(jnp.sum(weights, axis=1)) + own_weight
    probs = weights.astype(jnp.bfloat16)
    own_prob = own_weight.astype(jnp.bfloat16)
    summed = jnp.dot(probs, value_block, preferred_element_type=jnp.float32)
    summed = summed + own_prob.astype(jnp.float32)[:, None] * fresh_value.astype(jnp.float32)[None, :]
    return (summed / total[:, None]).astype(jnp.bfloat16)

def reference(hidden_in, norm_gain, w_query, w_key, w_value, w_out, key_cache, value_cache, lengths):
    widened = hidden_in.astype(jnp.float32)
    inverse = lax.rsqrt(lax.optimization_barrier(jnp.mean(widened * widened, axis=1)) + 1e-05)
    scaled = (widened * norm_gain.astype(jnp.float32)[None, :]).astype(jnp.bfloat16)
    query = (jnp.dot(scaled, w_query, preferred_element_type=jnp.float32) * inverse[:, None]).astype(jnp.bfloat16)
    new_key = (jnp.dot(scaled, w_key, preferred_element_type=jnp.float32) * inverse[:, None]).astype(jnp.bfloat16)
    new_value = (jnp.dot(scaled, w_value, preferred_element_type=jnp.float32) * inverse[:, None]).astype(jnp.bfloat16)
    query_slots = query.reshape(BATCH * KVH, G, HD)
    key_slots = new_key.reshape(BATCH * KVH, HD)
    value_slots = new_value.reshape(BATCH * KVH, HD)
    slot_lengths = jnp.repeat(lengths, KVH)

    def one_slot(items):
        return attend_slot(items[0], items[1], items[2], items[3], items[4], items[5])
    attended = lax.map(one_slot, (query_slots, key_cache, value_cache, key_slots, value_slots, slot_lengths))
    flat = attended.reshape(BATCH, KVH * G * HD)
    return jnp.dot(flat, w_out, preferred_element_type=jnp.float32).astype(jnp.bfloat16)
```

```python
import functools

import jax
import jax.numpy as jnp
from jax import lax
from jax.experimental import pallas as pl
from jax.experimental.pallas import tpu as pltpu
from jax.sharding import PartitionSpec as P

D = 16384
HD = 128
KVH = 4
G = 16


def attend_slot(query_heads, key_block, value_block, fresh_key, fresh_value, length):
    factor = HD ** (-0.5)
    scores = jnp.dot(query_heads, key_block.T, preferred_element_type=jnp.float32) * factor
    positions = jnp.arange(key_block.shape[0], dtype=jnp.int32)
    scores = jnp.where(positions[None, :] < length, scores, -jnp.inf)
    own_score = jnp.dot(query_heads, fresh_key, preferred_element_type=jnp.float32) * factor
    highest = jnp.maximum(jnp.max(scores, axis=1), own_score)
    weights = jnp.exp(scores - highest[:, None])
    own_weight = jnp.exp(own_score - highest)
    total = jnp.sum(weights, axis=1) + own_weight
    probs = weights.astype(jnp.bfloat16)
    own_prob = own_weight.astype(jnp.bfloat16)
    summed = jnp.dot(probs, value_block, preferred_element_type=jnp.float32)
    summed = (
        summed + own_prob.astype(jnp.float32)[:, None] * fresh_value.astype(jnp.float32)[None, :]
    )
    return (summed / total[:, None]).astype(jnp.bfloat16)


def local(hidden_in, norm_gain, w_query, w_key, w_value, w_out, key_cache, value_cache, lengths):
    batch = hidden_in.shape[0]
    slots_here = key_cache.shape[0]
    first_slot = lax.axis_index("wx") * slots_here
    widened = hidden_in.astype(jnp.float32)
    squares = lax.psum(jnp.sum(widened * widened, axis=1), "wx")
    inverse = lax.rsqrt(squares / D + 1e-05)
    slot_inverse = jnp.repeat(inverse, KVH)
    scaled = (widened * norm_gain.astype(jnp.float32)[None, :]).astype(jnp.bfloat16)
    query_part = jnp.dot(scaled, w_query, preferred_element_type=jnp.float32).reshape(
        batch, KVH, G * HD
    )
    key_part = jnp.dot(scaled, w_key, preferred_element_type=jnp.float32).reshape(batch, KVH, HD)
    value_part = jnp.dot(scaled, w_value, preferred_element_type=jnp.float32).reshape(
        batch, KVH, HD
    )
    terms = jnp.concatenate([query_part, key_part, value_part], axis=2).reshape(
        batch * KVH, (G + 2) * HD
    )
    scaled_terms = terms * slot_inverse[:, None]
    reduced = lax.psum_scatter(scaled_terms, "wx", scatter_dimension=0, tiled=True)
    query = reduced[:, : G * HD].astype(jnp.bfloat16).reshape(slots_here, G, HD)
    new_key = reduced[:, G * HD : (G + 1) * HD].astype(jnp.bfloat16)
    new_value = reduced[:, (G + 1) * HD :].astype(jnp.bfloat16)
    row_ids = (first_slot + jnp.arange(slots_here, dtype=jnp.int32)) // KVH
    slot_lengths = jnp.take(lengths, row_ids)
    attended = jax.vmap(attend_slot)(
        query, key_cache, value_cache, new_key, new_value, slot_lengths
    )
    gathered = lax.all_gather(attended.reshape(slots_here, G * HD), "wx", axis=0, tiled=True)
    flat = gathered.reshape(batch, KVH * G * HD)
    rows_here = w_out.shape[0]
    mine = lax.dynamic_slice_in_dim(flat, lax.axis_index("wx") * rows_here, rows_here, 1)
    partial_out = jnp.dot(mine, w_out, preferred_element_type=jnp.float32)
    block_out = lax.psum_scatter(partial_out, "wx", scatter_dimension=1, tiled=True).astype(
        jnp.bfloat16
    )
    return block_out


MSG = 24
QCOLS = 1024
SCORE_BLOCK = 2048


def fused_kernel(
    n, batch, hidden_ref, gain_ref, lengths_ref, wq_hbm, wk_hbm, wv_hbm, wo_hbm, kc_hbm, vc_hbm,
    out_ref, wq, wkv, wo, kc, vc, terms, terms_in, scores, att_out, att_in, parts_out, parts_in,
    own_part, wq_sem, wkv_sem, wo_sem, cache_sem, a_send, a_recv, c_send, c_recv, d_send, d_recv,
):
    me = lax.axis_index("wx")
    my_row = me // KVH
    my_head = me % KVH
    halves = G * HD // QCOLS
    q_chunks = KVH * halves
    kv_cols = KVH * HD
    ctx = kc.shape[0]
    out_cols = wo.shape[1] // n
    blocks = out_cols // HD
    wo_rows = wo.shape[0]
    wo_piece = wo_rows // 4
    heads_here = wo_rows // HD

    def head_at(step):
        return (my_head + 1 + step) % KVH

    def key_weight_copy():
        return pltpu.make_async_copy(wk_hbm, wkv.at[:, pl.ds(0, kv_cols)], wkv_sem.at[0])

    def value_weight_copy():
        return pltpu.make_async_copy(wv_hbm, wkv.at[:, pl.ds(kv_cols, kv_cols)], wkv_sem.at[1])

    def query_weight_copy(step, half):
        start = pl.multiple_of(head_at(step) * (G * HD) + half * QCOLS, QCOLS)
        chunk = step * halves + half
        return pltpu.make_async_copy(
            wq_hbm.at[:, pl.ds(start, QCOLS)], wq.at[chunk], wq_sem.at[chunk]
        )

    def cache_copy(which):
        source, target = ((kc_hbm, kc), (vc_hbm, vc))[which]
        return pltpu.make_async_copy(source.at[0], target, cache_sem.at[which])

    def out_weight_copy(piece):
        rows = pl.ds(piece * wo_piece, wo_piece)
        return pltpu.make_async_copy(wo_hbm.at[rows], wo.at[rows], wo_sem.at[piece])

    key_weight_copy().start()
    value_weight_copy().start()
    for chunk in range(q_chunks):
        query_weight_copy(chunk // halves, chunk % halves).start()

    barrier = pltpu.get_barrier_semaphore()

    def greet(k, carry):
        pl.semaphore_signal(
            barrier, inc=1, device_id={"wx": (me + k) % n}, device_id_type=pl.DeviceIdType.MESH
        )
        return carry

    lax.fori_loop(1, n, greet, 0)

    widened = hidden_ref[...].astype(jnp.float32)
    scaled = (widened * gain_ref[...].astype(jnp.float32)).astype(jnp.bfloat16)
    squares = jnp.broadcast_to(jnp.sum(widened * widened, axis=1, keepdims=True), (batch, HD))
    terms[...] = jnp.zeros_like(terms)
    for head in range(KVH):
        terms[pl.ds(head * MSG + G + 2, batch, stride=KVH * MSG), :] = squares

    key_weight_copy().wait()
    value_weight_copy().wait()
    fresh = jnp.dot(scaled, wkv[...], preferred_element_type=jnp.float32)
    for head in range(KVH):
        for which in range(2):
            column = which * kv_cols + head * HD
            terms[pl.ds(head * MSG + G + which, batch, stride=KVH * MSG), :] = fresh[
                :, column : column + HD
            ]

    pl.semaphore_wait(barrier, n - 1)

    def terms_copy(target):
        place = (me - target + n) % n - 1
        return pltpu.make_async_remote_copy(
            src_ref=terms.at[pl.ds(pl.multiple_of(target * MSG, MSG), MSG)],
            dst_ref=terms_in.at[place],
            send_sem=a_send,
            recv_sem=a_recv,
            device_id={"wx": target},
            device_id_type=pl.DeviceIdType.MESH,
        )

    for step in range(KVH):
        head = head_at(step)
        for half in range(halves):
            query_weight_copy(step, half).wait()
            chunk = step * halves + half
            if chunk == q_chunks - 4:
                cache_copy(0).start()
            if chunk == q_chunks - 3:
                cache_copy(1).start()
            if chunk >= q_chunks - 2:
                first = 2 * (chunk - q_chunks + 2)
                out_weight_copy(first).start()
                out_weight_copy(first + 1).start()
            part = jnp.dot(scaled, wq[chunk], preferred_element_type=jnp.float32)
            for j in range(QCOLS // HD):
                row = head * MSG + half * (QCOLS // HD) + j
                terms[pl.ds(row, batch, stride=KVH * MSG), :] = part[:, j * HD : (j + 1) * HD]
        for row in range(batch):
            target = row * KVH + head

            @pl.when(target != me)
            def _():
                terms_copy(target).start()

    def all_terms():
        return pltpu.make_async_remote_copy(
            src_ref=terms_in,
            dst_ref=terms_in,
            send_sem=a_send,
            recv_sem=a_recv,
            device_id={"wx": (me + 1) % n},
            device_id_type=pl.DeviceIdType.MESH,
        )

    cache_copy(0).wait()
    all_terms().wait_recv()
    total_terms = terms[pl.ds(pl.multiple_of(me * MSG, MSG), MSG), :]
    for k in range(n - 1):
        total_terms = total_terms + terms_in[k]
    inverse = lax.rsqrt(total_terms[G + 2 : G + 3] / D + 1e-05)
    rounded = (total_terms[: G + 2] * inverse).astype(jnp.bfloat16)
    query = rounded[:G]
    new_key = rounded[G : G + 1].astype(jnp.float32)
    new_value = rounded[G + 1 : G + 2].astype(jnp.float32)

    factor = HD ** (-0.5)
    length = lengths_ref[my_row]
    own_score = jnp.sum(query.astype(jnp.float32) * new_key, axis=1, keepdims=True) * factor
    highest = own_score
    for c in range(ctx // SCORE_BLOCK):
        span = pl.ds(c * SCORE_BLOCK, SCORE_BLOCK)
        piece = lax.dot_general(
            query, kc[span, :], (((1,), (1,)), ((), ())), preferred_element_type=jnp.float32
        ) * factor
        positions = lax.broadcasted_iota(jnp.int32, piece.shape, 1) + c * SCORE_BLOCK
        piece = jnp.where(positions < length, piece, -jnp.inf)
        scores[:, span] = piece
        highest = jnp.maximum(highest, jnp.max(piece, axis=1, keepdims=True))
    own_weight = jnp.exp(own_score - highest)
    total = own_weight
    summed = own_weight.astype(jnp.bfloat16).astype(jnp.float32) * new_value
    cache_copy(1).wait()
    for c in range(ctx // SCORE_BLOCK):
        span = pl.ds(c * SCORE_BLOCK, SCORE_BLOCK)
        weights = jnp.exp(scores[:, span] - highest)
        total = total + jnp.sum(weights, axis=1, keepdims=True)
        summed = summed + jnp.dot(
            weights.astype(jnp.bfloat16), vc[span, :], preferred_element_type=jnp.float32
        )
    attended = (summed / total).astype(jnp.bfloat16).astype(jnp.float32)

    sharers = G // heads_here
    for i in range(sharers):
        att_out[i, :heads_here] = attended[i * heads_here : (i + 1) * heads_here]

    def attended_copy(i, row, target):
        return pltpu.make_async_remote_copy(
            src_ref=att_out.at[i],
            dst_ref=att_in.at[row],
            send_sem=c_send.at[i],
            recv_sem=c_recv.at[row],
            device_id={"wx": target},
            device_id_type=pl.DeviceIdType.MESH,
        )

    for i in range(sharers):
        target = my_head * sharers + i

        @pl.when(target != me)
        def _():
            attended_copy(i, my_row, target).start()

        @pl.when(target == me)
        def _():
            att_in[my_row] = att_out[i]

    for piece in range(4):
        out_weight_copy(piece).wait()
    for row in range(batch):
        source = row * KVH + me // sharers

        @pl.when(source != me)
        def _():
            attended_copy(0, row, source).wait_recv()

    everything = att_in[...]
    mine = jnp.concatenate([everything[:, j] for j in range(heads_here)], axis=1).astype(
        jnp.bfloat16
    )

    def product(target):
        start = pl.multiple_of(target * out_cols, out_cols)
        part = jnp.dot(mine, wo[:, pl.ds(start, out_cols)], preferred_element_type=jnp.float32)
        return jnp.concatenate([part[:, b * HD : (b + 1) * HD] for b in range(blocks)], axis=0)

    def send_part(i, carry):
        k = n // 2 + (1 - 2 * (i % 2)) * ((i + 1) // 2)
        target = (me + k) % n
        parts_out[k - 1] = product(target).astype(jnp.bfloat16)
        pltpu.make_async_remote_copy(
            src_ref=parts_out.at[k - 1],
            dst_ref=parts_in.at[k - 1],
            send_sem=d_send,
            recv_sem=d_recv,
            device_id={"wx": target},
            device_id_type=pl.DeviceIdType.MESH,
        ).start()
        return carry

    lax.fori_loop(0, n - 1, send_part, 0)
    result = product(me)
    all_parts = pltpu.make_async_remote_copy(
        src_ref=parts_out,
        dst_ref=parts_in,
        send_sem=d_send,
        recv_sem=d_recv,
        device_id={"wx": (me + 1) % n},
        device_id_type=pl.DeviceIdType.MESH,
    )
    all_parts.wait_recv()
    for k in range(n - 1):
        result = result + parts_in[k].astype(jnp.float32)
    out_ref[...] = jnp.concatenate(
        [result[b * batch : (b + 1) * batch] for b in range(blocks)], axis=1
    ).astype(jnp.bfloat16)

    all_parts.wait_send()
    all_terms().wait_send()
    for i in range(sharers):
        target = my_head * sharers + i

        @pl.when(target != me)
        def _():
            attended_copy(i, my_row, target).wait_send()


def fused(n, hidden_in, norm_gain, w_query, w_key, w_value, w_out, key_cache, value_cache, lengths):
    batch, features = hidden_in.shape
    ctx = key_cache.shape[1]
    out_cols = w_out.shape[1] // n
    part_rows = batch * out_cols // HD
    q_chunks = w_query.shape[1] // QCOLS
    vmem = pl.BlockSpec(memory_space=pltpu.VMEM)
    hbm = pl.BlockSpec(memory_space=pl.ANY)
    smem = pl.BlockSpec(memory_space=pltpu.SMEM)
    bf16, f32 = jnp.bfloat16, jnp.float32
    return pl.pallas_call(
        functools.partial(fused_kernel, n, batch),
        out_shape=jax.ShapeDtypeStruct((batch, out_cols), bf16),
        in_specs=[vmem, vmem, smem] + [hbm] * 6,
        out_specs=vmem,
        scratch_shapes=[
            pltpu.VMEM((q_chunks, features, QCOLS), bf16),
            pltpu.VMEM((features, 2 * KVH * HD), bf16),
            pltpu.VMEM(w_out.shape, bf16),
            pltpu.VMEM((ctx, HD), bf16),
            pltpu.VMEM((ctx, HD), bf16),
            pltpu.VMEM((n * MSG, HD), f32),
            pltpu.VMEM((n - 1, MSG, HD), f32),
            pltpu.VMEM((G, ctx), f32),
            pltpu.VMEM((G * HD // w_out.shape[0], 8, HD), f32),
            pltpu.VMEM((batch, 8, HD), f32),
            pltpu.VMEM((n - 1, part_rows, HD), bf16),
            pltpu.VMEM((n - 1, part_rows, HD), bf16),
            pltpu.VMEM((part_rows, HD), f32),
            pltpu.SemaphoreType.DMA((q_chunks,)),
            pltpu.SemaphoreType.DMA((2,)),
            pltpu.SemaphoreType.DMA((4,)),
            pltpu.SemaphoreType.DMA((2,)),
            pltpu.SemaphoreType.DMA,
            pltpu.SemaphoreType.DMA,
            pltpu.SemaphoreType.DMA((G * HD // w_out.shape[0],)),
            pltpu.SemaphoreType.DMA((batch,)),
            pltpu.SemaphoreType.DMA,
            pltpu.SemaphoreType.DMA,
        ],
        compiler_params=pltpu.CompilerParams(
            collective_id=0, has_side_effects=True, vmem_limit_bytes=56 * 1024 * 1024
        ),
    )(
        hidden_in, norm_gain.reshape(1, features), lengths, w_query, w_key, w_value, w_out,
        key_cache, value_cache,
    )


def choose(n, *arrays):
    hidden_in, w_out, key_cache = arrays[0], arrays[5], arrays[6]
    rows_here = w_out.shape[0]
    fits = (
        key_cache.shape[0] == 1
        and hidden_in.shape[0] * KVH == n
        and rows_here % HD == 0
        and (G * HD) % rows_here == 0
        and rows_here <= 8 * HD
        and key_cache.shape[1] % SCORE_BLOCK == 0
        and (hidden_in.shape[0] * (w_out.shape[1] // n // HD)) % 16 == 0
    )
    return fused(n, *arrays) if fits else local(*arrays)


def solution(mesh):
    in_specs = (
        P("group", "wx"),
        P("wx"),
        P("wx", None),
        P("wx", None),
        P("wx", None),
        P("wx", None),
        P(("group", "wx"), None, None),
        P(("group", "wx"), None, None),
        P("group"),
    )
    out_specs = P("group", "wx")
    return jax.shard_map(
        functools.partial(choose, mesh.shape["wx"]), mesh=mesh, in_specs=in_specs, out_specs=out_specs, check_vma=False)
```

```python
import functools

import jax
import jax.numpy as jnp
from jax import lax
from jax.experimental import pallas as pl
from jax.experimental.pallas import tpu as pltpu
from jax.sharding import PartitionSpec as P

D = 16384
HD = 128
KVH = 4
G = 16


def attend_slot(query_heads, key_block, value_block, fresh_key, fresh_value, length):
    factor = HD ** (-0.5)
    scores = jnp.dot(query_heads, key_block.T, preferred_element_type=jnp.float32) * factor
    positions = jnp.arange(key_block.shape[0], dtype=jnp.int32)
    scores = jnp.where(positions[None, :] < length, scores, -jnp.inf)
    own_score = jnp.dot(query_heads, fresh_key, preferred_element_type=jnp.float32) * factor
    highest = jnp.maximum(jnp.max(scores, axis=1), own_score)
    weights = jnp.exp(scores - highest[:, None])
    own_weight = jnp.exp(own_score - highest)
    total = jnp.sum(weights, axis=1) + own_weight
    probs = weights.astype(jnp.bfloat16)
    own_prob = own_weight.astype(jnp.bfloat16)
    summed = jnp.dot(probs, value_block, preferred_element_type=jnp.float32)
    summed = (
        summed + own_prob.astype(jnp.float32)[:, None] * fresh_value.astype(jnp.float32)[None, :]
    )
    return (summed / total[:, None]).astype(jnp.bfloat16)


def local(hidden_in, norm_gain, w_query, w_key, w_value, w_out, key_cache, value_cache, lengths):
    batch = hidden_in.shape[0]
    slots_here = key_cache.shape[0]
    first_slot = lax.axis_index("wx") * slots_here
    widened = hidden_in.astype(jnp.float32)
    squares = lax.psum(jnp.sum(widened * widened, axis=1), "wx")
    inverse = lax.rsqrt(squares / D + 1e-05)
    slot_inverse = jnp.repeat(inverse, KVH)
    scaled = (widened * norm_gain.astype(jnp.float32)[None, :]).astype(jnp.bfloat16)
    query_part = jnp.dot(scaled, w_query, preferred_element_type=jnp.float32).reshape(
        batch, KVH, G * HD
    )
    key_part = jnp.dot(scaled, w_key, preferred_element_type=jnp.float32).reshape(batch, KVH, HD)
    value_part = jnp.dot(scaled, w_value, preferred_element_type=jnp.float32).reshape(
        batch, KVH, HD
    )
    terms = jnp.concatenate([query_part, key_part, value_part], axis=2).reshape(
        batch * KVH, (G + 2) * HD
    )
    scaled_terms = terms * slot_inverse[:, None]
    reduced = lax.psum_scatter(scaled_terms, "wx", scatter_dimension=0, tiled=True)
    query = reduced[:, : G * HD].astype(jnp.bfloat16).reshape(slots_here, G, HD)
    new_key = reduced[:, G * HD : (G + 1) * HD].astype(jnp.bfloat16)
    new_value = reduced[:, (G + 1) * HD :].astype(jnp.bfloat16)
    row_ids = (first_slot + jnp.arange(slots_here, dtype=jnp.int32)) // KVH
    slot_lengths = jnp.take(lengths, row_ids)
    attended = jax.vmap(attend_slot)(
        query, key_cache, value_cache, new_key, new_value, slot_lengths
    )
    gathered = lax.all_gather(attended.reshape(slots_here, G * HD), "wx", axis=0, tiled=True)
    flat = gathered.reshape(batch, KVH * G * HD)
    rows_here = w_out.shape[0]
    mine = lax.dynamic_slice_in_dim(flat, lax.axis_index("wx") * rows_here, rows_here, 1)
    partial_out = jnp.dot(mine, w_out, preferred_element_type=jnp.float32)
    block_out = lax.psum_scatter(partial_out, "wx", scatter_dimension=1, tiled=True).astype(
        jnp.bfloat16
    )
    return block_out


MSG = 24
QCOLS = 1024
SCORE_BLOCK = 2048
IN_FLIGHT = 4
WO_PIECES = 8


def fused_kernel(
    n, batch, hidden_ref, gain_ref, lengths_ref, wq_hbm, wk_hbm, wv_hbm, wo_hbm, kc_hbm, vc_hbm,
    out_ref, wq, wkv, wo, kc, vc, terms, terms_in, scores, att_out, att_in, parts_out, parts_in,
    wq_sem, wkv_sem, wo_sem, cache_sem, a_send, a_recv, c_send, c_recv, d_send, d_recv,
):
    me = lax.axis_index("wx")
    my_row = me // KVH
    my_head = me % KVH
    halves = G * HD // QCOLS
    q_chunks = KVH * halves
    kv_cols = KVH * HD
    ctx = kc.shape[0]
    out_cols = wo.shape[1] // n
    blocks = out_cols // HD
    wo_rows = wo.shape[0]
    wo_pieces = wo_sem.shape[0]
    wo_piece = wo_rows // wo_pieces
    heads_here = wo_rows // HD

    def head_at(step):
        return (my_head + 1 + step) % KVH

    def key_weight_copy():
        return pltpu.make_async_copy(wk_hbm, wkv.at[:, pl.ds(0, kv_cols)], wkv_sem.at[0])

    def value_weight_copy():
        return pltpu.make_async_copy(wv_hbm, wkv.at[:, pl.ds(kv_cols, kv_cols)], wkv_sem.at[1])

    def query_weight_copy(step, half):
        start = pl.multiple_of(head_at(step) * (G * HD) + half * QCOLS, QCOLS)
        chunk = step * halves + half
        return pltpu.make_async_copy(
            wq_hbm.at[:, pl.ds(start, QCOLS)], wq.at[chunk], wq_sem.at[chunk]
        )

    def cache_copy(which):
        source, target = ((kc_hbm, kc), (vc_hbm, vc))[which]
        return pltpu.make_async_copy(source.at[0], target, cache_sem.at[which])

    def out_weight_copy(piece):
        rows = pl.ds(piece * wo_piece, wo_piece)
        return pltpu.make_async_copy(wo_hbm.at[rows], wo.at[rows], wo_sem.at[piece])

    stream = [key_weight_copy, value_weight_copy]
    stream += [
        functools.partial(query_weight_copy, chunk // halves, chunk % halves)
        for chunk in range(q_chunks)
    ]
    stream += [functools.partial(cache_copy, which) for which in range(2)]
    stream += [functools.partial(out_weight_copy, piece) for piece in range(wo_pieces)]

    def start_next(count):
        for _ in range(count):
            if stream:
                stream.pop(0)().start()

    start_next(2 + IN_FLIGHT)

    barrier = pltpu.get_barrier_semaphore()

    def greet(k, carry):
        pl.semaphore_signal(
            barrier, inc=1, device_id={"wx": (me + k) % n}, device_id_type=pl.DeviceIdType.MESH
        )
        return carry

    lax.fori_loop(1, n, greet, 0)

    widened = hidden_ref[...].astype(jnp.float32)
    scaled = (widened * gain_ref[...].astype(jnp.float32).reshape(1, -1)).astype(jnp.bfloat16)
    squares = jnp.broadcast_to(jnp.sum(widened * widened, axis=1, keepdims=True), (batch, HD))
    terms[...] = jnp.zeros_like(terms)
    for head in range(KVH):
        terms[pl.ds(head * MSG + G + 2, batch, stride=KVH * MSG), :] = squares

    key_weight_copy().wait()
    value_weight_copy().wait()
    fresh = jnp.dot(scaled, wkv[...], preferred_element_type=jnp.float32)
    for head in range(KVH):
        for which in range(2):
            column = which * kv_cols + head * HD
            terms[pl.ds(head * MSG + G + which, batch, stride=KVH * MSG), :] = fresh[
                :, column : column + HD
            ]

    pl.semaphore_wait(barrier, n - 1)

    def terms_copy(target):
        place = (me - target + n) % n - 1
        return pltpu.make_async_remote_copy(
            src_ref=terms.at[pl.ds(pl.multiple_of(target * MSG, MSG), MSG)],
            dst_ref=terms_in.at[place],
            send_sem=a_send,
            recv_sem=a_recv,
            device_id={"wx": target},
            device_id_type=pl.DeviceIdType.MESH,
        )

    for step in range(KVH):
        head = head_at(step)
        for half in range(halves):
            query_weight_copy(step, half).wait()
            chunk = step * halves + half
            start_next(1)
            part = jnp.dot(scaled, wq[chunk], preferred_element_type=jnp.float32)
            for j in range(QCOLS // HD):
                row = head * MSG + half * (QCOLS // HD) + j
                terms[pl.ds(row, batch, stride=KVH * MSG), :] = part[:, j * HD : (j + 1) * HD]
        for row in range(batch):
            target = row * KVH + head

            @pl.when(target != me)
            def _():
                terms_copy(target).start()

    def all_terms():
        return pltpu.make_async_remote_copy(
            src_ref=terms_in,
            dst_ref=terms_in,
            send_sem=a_send,
            recv_sem=a_recv,
            device_id={"wx": (me + 1) % n},
            device_id_type=pl.DeviceIdType.MESH,
        )

    for which in range(2):
        cache_copy(which).wait()
        start_next(2)
    start_next(wo_pieces)
    all_terms().wait_recv()
    total_terms = terms[pl.ds(pl.multiple_of(me * MSG, MSG), MSG), :]
    for k in range(n - 1):
        total_terms = total_terms + terms_in[k]
    inverse = lax.rsqrt(total_terms[G + 2 : G + 3] / D + 1e-05)
    rounded = (total_terms[: G + 2] * inverse).astype(jnp.bfloat16)
    query = rounded[:G]
    new_key = rounded[G : G + 1].astype(jnp.float32)
    new_value = rounded[G + 1 : G + 2].astype(jnp.float32)

    factor = HD ** (-0.5)
    length = lengths_ref[my_row]
    own_score = jnp.sum(query.astype(jnp.float32) * new_key, axis=1, keepdims=True) * factor
    highest = own_score
    for c in range(ctx // SCORE_BLOCK):
        span = pl.ds(c * SCORE_BLOCK, SCORE_BLOCK)
        piece = lax.dot_general(
            query, kc[span, :], (((1,), (1,)), ((), ())), preferred_element_type=jnp.float32
        ) * factor
        positions = lax.broadcasted_iota(jnp.int32, piece.shape, 1) + c * SCORE_BLOCK
        piece = jnp.where(positions < length, piece, -jnp.inf)
        scores[:, span] = piece
        highest = jnp.maximum(highest, jnp.max(piece, axis=1, keepdims=True))
    own_weight = jnp.exp(own_score - highest)
    total = own_weight
    summed = own_weight.astype(jnp.bfloat16).astype(jnp.float32) * new_value
    for c in range(ctx // SCORE_BLOCK):
        span = pl.ds(c * SCORE_BLOCK, SCORE_BLOCK)
        weights = jnp.exp(scores[:, span] - highest)
        total = total + jnp.sum(weights, axis=1, keepdims=True)
        summed = summed + jnp.dot(
            weights.astype(jnp.bfloat16), vc[span, :], preferred_element_type=jnp.float32
        )
    attended = (summed / total).astype(jnp.bfloat16).astype(jnp.float32)

    sharers = G // heads_here
    for i in range(sharers):
        att_out[i, :heads_here] = attended[i * heads_here : (i + 1) * heads_here]

    def attended_copy(i, row, target):
        return pltpu.make_async_remote_copy(
            src_ref=att_out.at[i],
            dst_ref=att_in.at[row],
            send_sem=c_send.at[i],
            recv_sem=c_recv.at[row],
            device_id={"wx": target},
            device_id_type=pl.DeviceIdType.MESH,
        )

    for i in range(sharers):
        target = my_head * sharers + i

        @pl.when(target != me)
        def _():
            attended_copy(i, my_row, target).start()

        @pl.when(target == me)
        def _():
            att_in[my_row] = att_out[i]

    for piece in range(wo_pieces):
        out_weight_copy(piece).wait()
    for row in range(batch):
        source = row * KVH + me // sharers

        @pl.when(source != me)
        def _():
            attended_copy(0, row, source).wait_recv()

    everything = att_in[...]
    mine = jnp.concatenate([everything[:, j] for j in range(heads_here)], axis=1).astype(
        jnp.bfloat16
    )

    def product(target):
        start = pl.multiple_of(target * out_cols, out_cols)
        part = jnp.dot(mine, wo[:, pl.ds(start, out_cols)], preferred_element_type=jnp.float32)
        return jnp.concatenate([part[:, b * HD : (b + 1) * HD] for b in range(blocks)], axis=0)

    def send_part(i, carry):
        k = n // 2 + (1 - 2 * (i % 2)) * ((i + 1) // 2)
        target = (me + k) % n
        parts_out[k - 1] = product(target).astype(jnp.bfloat16)
        pltpu.make_async_remote_copy(
            src_ref=parts_out.at[k - 1],
            dst_ref=parts_in.at[k - 1],
            send_sem=d_send,
            recv_sem=d_recv,
            device_id={"wx": target},
            device_id_type=pl.DeviceIdType.MESH,
        ).start()
        return carry

    lax.fori_loop(0, n - 1, send_part, 0)
    result = product(me)
    all_parts = pltpu.make_async_remote_copy(
        src_ref=parts_out,
        dst_ref=parts_in,
        send_sem=d_send,
        recv_sem=d_recv,
        device_id={"wx": (me + 1) % n},
        device_id_type=pl.DeviceIdType.MESH,
    )
    all_parts.wait_recv()
    for k in range(n - 1):
        result = result + parts_in[k].astype(jnp.float32)
    out_ref[...] = jnp.concatenate(
        [result[b * batch : (b + 1) * batch] for b in range(blocks)], axis=1
    ).astype(jnp.bfloat16)

    all_parts.wait_send()
    all_terms().wait_send()
    for i in range(sharers):
        target = my_head * sharers + i

        @pl.when(target != me)
        def _():
            attended_copy(i, my_row, target).wait_send()


def fused(n, hidden_in, norm_gain, w_query, w_key, w_value, w_out, key_cache, value_cache, lengths):
    batch, features = hidden_in.shape
    ctx = key_cache.shape[1]
    out_cols = w_out.shape[1] // n
    part_rows = batch * out_cols // HD
    q_chunks = w_query.shape[1] // QCOLS
    vmem = pl.BlockSpec(memory_space=pltpu.VMEM)
    hbm = pl.BlockSpec(memory_space=pl.ANY)
    smem = pl.BlockSpec(memory_space=pltpu.SMEM)
    bf16, f32 = jnp.bfloat16, jnp.float32
    return pl.pallas_call(
        functools.partial(fused_kernel, n, batch),
        out_shape=jax.ShapeDtypeStruct((batch, out_cols), bf16),
        in_specs=[vmem, vmem, smem] + [hbm] * 6,
        out_specs=vmem,
        scratch_shapes=[
            pltpu.VMEM((q_chunks, features, QCOLS), bf16),
            pltpu.VMEM((features, 2 * KVH * HD), bf16),
            pltpu.VMEM(w_out.shape, bf16),
            pltpu.VMEM((ctx, HD), bf16),
            pltpu.VMEM((ctx, HD), bf16),
            pltpu.VMEM((n * MSG, HD), f32),
            pltpu.VMEM((n - 1, MSG, HD), f32),
            pltpu.VMEM((G, ctx), f32),
            pltpu.VMEM((G * HD // w_out.shape[0], 8, HD), f32),
            pltpu.VMEM((batch, 8, HD), f32),
            pltpu.VMEM((n - 1, part_rows, HD), bf16),
            pltpu.VMEM((n - 1, part_rows, HD), bf16),
            pltpu.SemaphoreType.DMA((q_chunks,)),
            pltpu.SemaphoreType.DMA((2,)),
            pltpu.SemaphoreType.DMA((WO_PIECES,)),
            pltpu.SemaphoreType.DMA((2,)),
            pltpu.SemaphoreType.DMA,
            pltpu.SemaphoreType.DMA,
            pltpu.SemaphoreType.DMA((G * HD // w_out.shape[0],)),
            pltpu.SemaphoreType.DMA((batch,)),
            pltpu.SemaphoreType.DMA,
            pltpu.SemaphoreType.DMA,
        ],
        compiler_params=pltpu.CompilerParams(
            collective_id=0, has_side_effects=True, vmem_limit_bytes=56 * 1024 * 1024
        ),
    )(
        hidden_in, norm_gain, lengths, w_query, w_key, w_value, w_out,
        key_cache, value_cache,
    )


def choose(n, *arrays):
    hidden_in, w_out, key_cache = arrays[0], arrays[5], arrays[6]
    rows_here = w_out.shape[0]
    fits = (
        key_cache.shape[0] == 1
        and hidden_in.shape[0] * KVH == n
        and rows_here % HD == 0
        and (G * HD) % rows_here == 0
        and rows_here <= 8 * HD
        and rows_here % (16 * WO_PIECES) == 0
        and key_cache.shape[1] % SCORE_BLOCK == 0
        and (hidden_in.shape[0] * (w_out.shape[1] // n // HD)) % 16 == 0
    )
    return fused(n, *arrays) if fits else local(*arrays)


def solution(mesh):
    in_specs = (
        P("group", "wx"),
        P("wx"),
        P("wx", None),
        P("wx", None),
        P("wx", None),
        P("wx", None),
        P(("group", "wx"), None, None),
        P(("group", "wx"), None, None),
        P("group"),
    )
    out_specs = P("group", "wx")
    return jax.shard_map(
        functools.partial(choose, mesh.shape["wx"]), mesh=mesh, in_specs=in_specs, out_specs=out_specs, check_vma=False)
```

```python
import functools

import jax
import jax.numpy as jnp
from jax import lax
from jax.experimental import pallas as pl
from jax.experimental.pallas import tpu as pltpu
from jax.sharding import PartitionSpec as P

D = 16384
HD = 128
KVH = 4
G = 16


def attend_slot(query_heads, key_block, value_block, fresh_key, fresh_value, length):
    factor = HD ** (-0.5)
    scores = jnp.dot(query_heads, key_block.T, preferred_element_type=jnp.float32) * factor
    positions = jnp.arange(key_block.shape[0], dtype=jnp.int32)
    scores = jnp.where(positions[None, :] < length, scores, -jnp.inf)
    own_score = jnp.dot(query_heads, fresh_key, preferred_element_type=jnp.float32) * factor
    highest = jnp.maximum(jnp.max(scores, axis=1), own_score)
    weights = jnp.exp(scores - highest[:, None])
    own_weight = jnp.exp(own_score - highest)
    total = jnp.sum(weights, axis=1) + own_weight
    probs = weights.astype(jnp.bfloat16)
    own_prob = own_weight.astype(jnp.bfloat16)
    summed = jnp.dot(probs, value_block, preferred_element_type=jnp.float32)
    summed = (
        summed + own_prob.astype(jnp.float32)[:, None] * fresh_value.astype(jnp.float32)[None, :]
    )
    return (summed / total[:, None]).astype(jnp.bfloat16)


def local(hidden_in, norm_gain, w_query, w_key, w_value, w_out, key_cache, value_cache, lengths):
    batch = hidden_in.shape[0]
    slots_here = key_cache.shape[0]
    first_slot = lax.axis_index("wx") * slots_here
    widened = hidden_in.astype(jnp.float32)
    squares = lax.psum(jnp.sum(widened * widened, axis=1), "wx")
    inverse = lax.rsqrt(squares / D + 1e-05)
    slot_inverse = jnp.repeat(inverse, KVH)
    scaled = (widened * norm_gain.astype(jnp.float32)[None, :]).astype(jnp.bfloat16)
    query_part = jnp.dot(scaled, w_query, preferred_element_type=jnp.float32).reshape(
        batch, KVH, G * HD
    )
    key_part = jnp.dot(scaled, w_key, preferred_element_type=jnp.float32).reshape(batch, KVH, HD)
    value_part = jnp.dot(scaled, w_value, preferred_element_type=jnp.float32).reshape(
        batch, KVH, HD
    )
    terms = jnp.concatenate([query_part, key_part, value_part], axis=2).reshape(
        batch * KVH, (G + 2) * HD
    )
    scaled_terms = terms * slot_inverse[:, None]
    reduced = lax.psum_scatter(scaled_terms, "wx", scatter_dimension=0, tiled=True)
    query = reduced[:, : G * HD].astype(jnp.bfloat16).reshape(slots_here, G, HD)
    new_key = reduced[:, G * HD : (G + 1) * HD].astype(jnp.bfloat16)
    new_value = reduced[:, (G + 1) * HD :].astype(jnp.bfloat16)
    row_ids = (first_slot + jnp.arange(slots_here, dtype=jnp.int32)) // KVH
    slot_lengths = jnp.take(lengths, row_ids)
    attended = jax.vmap(attend_slot)(
        query, key_cache, value_cache, new_key, new_value, slot_lengths
    )
    gathered = lax.all_gather(attended.reshape(slots_here, G * HD), "wx", axis=0, tiled=True)
    flat = gathered.reshape(batch, KVH * G * HD)
    rows_here = w_out.shape[0]
    mine = lax.dynamic_slice_in_dim(flat, lax.axis_index("wx") * rows_here, rows_here, 1)
    partial_out = jnp.dot(mine, w_out, preferred_element_type=jnp.float32)
    block_out = lax.psum_scatter(partial_out, "wx", scatter_dimension=1, tiled=True).astype(
        jnp.bfloat16
    )
    return block_out


MSG = 24
SPLIT = 16
KEY_AT = 8
QCOLS = 1024
SCORE_BLOCK = 2048
IN_FLIGHT = 4
GREET_STEP = 1
HELD = 0
AFTER_TERMS = 2
AFTER_CACHE = 1
PACED = 0
WO_PIECES = 8


def fused_kernel(
    n, batch, hidden_ref, gain_ref, lengths_ref, wq_hbm, wk_hbm, wv_hbm, wo_hbm, kc_hbm, vc_hbm,
    out_ref, wq, wkv, wo, kc, vc, terms, terms_in, scores, att_out, att_in, parts_out, parts_in,
    wq_sem, wkv_sem, wo_sem, cache_sem, a_send, a_recv, c_send, c_recv, d_send, d_recv,
):
    me = lax.axis_index("wx")
    my_row = me // KVH
    my_head = me % KVH
    halves = G * HD // QCOLS
    q_chunks = KVH * halves
    kv_cols = KVH * HD
    ctx = kc.shape[0]
    out_cols = wo.shape[1] // n
    blocks = out_cols // HD
    wo_rows = wo.shape[0]
    wo_pieces = wo_sem.shape[0]
    wo_piece = wo_rows // wo_pieces
    heads_here = wo_rows // HD

    def head_at(step):
        return (my_head + 1 + step) % KVH

    def key_weight_copy():
        return pltpu.make_async_copy(wk_hbm, wkv.at[:, pl.ds(0, kv_cols)], wkv_sem.at[0])

    def value_weight_copy():
        return pltpu.make_async_copy(wv_hbm, wkv.at[:, pl.ds(kv_cols, kv_cols)], wkv_sem.at[1])

    def query_weight_copy(step, half):
        start = pl.multiple_of(head_at(step) * (G * HD) + half * QCOLS, QCOLS)
        chunk = step * halves + half
        return pltpu.make_async_copy(
            wq_hbm.at[:, pl.ds(start, QCOLS)], wq.at[chunk], wq_sem.at[chunk]
        )

    def cache_copy(which):
        source, target = ((kc_hbm, kc), (vc_hbm, vc))[which]
        return pltpu.make_async_copy(source.at[0], target, cache_sem.at[which])

    def out_weight_copy(piece):
        rows = pl.ds(piece * wo_piece, wo_piece)
        return pltpu.make_async_copy(wo_hbm.at[rows], wo.at[rows], wo_sem.at[piece])

    stream = [key_weight_copy, value_weight_copy]
    stream += [
        functools.partial(query_weight_copy, chunk // halves, chunk % halves)
        for chunk in range(q_chunks)
    ]
    stream += [functools.partial(cache_copy, which) for which in range(2)]
    stream += [functools.partial(out_weight_copy, piece) for piece in range(wo_pieces)]

    def start_next(count):
        for _ in range(count):
            if stream:
                stream.pop(0)().start()

    start_next(2 + IN_FLIGHT)

    barrier = pltpu.get_barrier_semaphore()

    def greet(k, carry):
        pl.semaphore_signal(
            barrier, inc=1, device_id={"wx": (me + k) % n}, device_id_type=pl.DeviceIdType.MESH
        )
        return carry

    lax.fori_loop(1, n, greet, 0)

    widened = hidden_ref[...].astype(jnp.float32)
    scaled = (widened * gain_ref[...].astype(jnp.float32).reshape(1, -1)).astype(jnp.bfloat16)
    squares = jnp.broadcast_to(jnp.sum(widened * widened, axis=1, keepdims=True), (batch, HD))
    terms[...] = jnp.zeros_like(terms)
    for head in range(KVH):
        terms[pl.ds(head * MSG + KEY_AT + 2, batch, stride=KVH * MSG), :] = squares

    key_weight_copy().wait()
    value_weight_copy().wait()
    fresh = jnp.dot(scaled, wkv[...], preferred_element_type=jnp.float32)
    for head in range(KVH):
        for which in range(2):
            column = which * kv_cols + head * HD
            terms[pl.ds(head * MSG + KEY_AT + which, batch, stride=KVH * MSG), :] = fresh[
                :, column : column + HD
            ]

    def terms_copy(target, half):
        place = (me - target + n) % n - 1
        rows = (SPLIT, MSG - SPLIT)[half]
        return pltpu.make_async_remote_copy(
            src_ref=terms.at[pl.ds(pl.multiple_of(target * MSG + half * SPLIT, 8), rows)],
            dst_ref=terms_in.at[place, pl.ds(half * SPLIT, rows)],
            send_sem=a_send,
            recv_sem=a_recv,
            device_id={"wx": target},
            device_id_type=pl.DeviceIdType.MESH,
        )

    ready = []
    for step in range(KVH):
        head = head_at(step)
        for half in range(halves):
            query_weight_copy(step, half).wait()
            chunk = step * halves + half
            if len(stream) > wo_pieces + HELD:
                start_next(1)
            part = jnp.dot(scaled, wq[chunk], preferred_element_type=jnp.float32)
            for j in range(QCOLS // HD):
                row = head * MSG + half * SPLIT + j
                terms[pl.ds(row, batch, stride=KVH * MSG), :] = part[:, j * HD : (j + 1) * HD]
            ready.append((head, half))
            if step == GREET_STEP and half == 0:
                pl.semaphore_wait(barrier, n - 1)
            if step >= GREET_STEP:
                for ready_head, ready_half in ready:
                    for row in range(batch):
                        target = row * KVH + ready_head

                        @pl.when(target != me)
                        def _():
                            terms_copy(target, ready_half).start()

                ready = []

    def all_terms():
        return pltpu.make_async_remote_copy(
            src_ref=terms_in,
            dst_ref=terms_in,
            send_sem=a_send,
            recv_sem=a_recv,
            device_id={"wx": (me + 1) % n},
            device_id_type=pl.DeviceIdType.MESH,
        )

    start_next(HELD + AFTER_TERMS)
    for which in range(2):
        cache_copy(which).wait()
        start_next(AFTER_CACHE)
    for piece in range(PACED):
        out_weight_copy(piece).wait()
        start_next(1)
    all_terms().wait_recv()
    start_next(wo_pieces)
    total_terms = terms[pl.ds(pl.multiple_of(me * MSG, MSG), MSG), :]
    for k in range(n - 1):
        total_terms = total_terms + terms_in[k]
    inverse = lax.rsqrt(total_terms[KEY_AT + 2 : KEY_AT + 3] / D + 1e-05)
    projected = total_terms * inverse
    query = jnp.concatenate([projected[:KEY_AT], projected[SPLIT:]], axis=0).astype(jnp.bfloat16)
    own_terms = projected[KEY_AT:SPLIT].astype(jnp.bfloat16).astype(jnp.float32)
    new_key = own_terms[0:1]
    new_value = own_terms[1:2]

    factor = HD ** (-0.5)
    length = lengths_ref[my_row]
    own_score = jnp.sum(query.astype(jnp.float32) * new_key, axis=1, keepdims=True) * factor
    highest = own_score
    for c in range(ctx // SCORE_BLOCK):
        span = pl.ds(c * SCORE_BLOCK, SCORE_BLOCK)
        piece = lax.dot_general(
            query, kc[span, :], (((1,), (1,)), ((), ())), preferred_element_type=jnp.float32
        ) * factor
        positions = lax.broadcasted_iota(jnp.int32, piece.shape, 1) + c * SCORE_BLOCK
        piece = jnp.where(positions < length, piece, -jnp.inf)
        scores[:, span] = piece
        highest = jnp.maximum(highest, jnp.max(piece, axis=1, keepdims=True))
    own_weight = jnp.exp(own_score - highest)
    total = own_weight
    summed = own_weight.astype(jnp.bfloat16).astype(jnp.float32) * new_value
    for c in range(ctx // SCORE_BLOCK):
        span = pl.ds(c * SCORE_BLOCK, SCORE_BLOCK)
        weights = jnp.exp(scores[:, span] - highest)
        total = total + jnp.sum(weights, axis=1, keepdims=True)
        summed = summed + jnp.dot(
            weights.astype(jnp.bfloat16), vc[span, :], preferred_element_type=jnp.float32
        )
    attended = (summed / total).astype(jnp.bfloat16).astype(jnp.float32)

    sharers = G // heads_here
    for i in range(sharers):
        att_out[i, :heads_here] = attended[i * heads_here : (i + 1) * heads_here]

    def attended_copy(i, row, target):
        return pltpu.make_async_remote_copy(
            src_ref=att_out.at[i],
            dst_ref=att_in.at[row],
            send_sem=c_send.at[i],
            recv_sem=c_recv.at[row],
            device_id={"wx": target},
            device_id_type=pl.DeviceIdType.MESH,
        )

    for i in range(sharers):
        target = my_head * sharers + i

        @pl.when(target != me)
        def _():
            attended_copy(i, my_row, target).start()

        @pl.when(target == me)
        def _():
            att_in[my_row] = att_out[i]

    for piece in range(PACED, wo_pieces):
        out_weight_copy(piece).wait()
    for row in range(batch):
        source = row * KVH + me // sharers

        @pl.when(source != me)
        def _():
            attended_copy(0, row, source).wait_recv()

    everything = att_in[...]
    mine = jnp.concatenate([everything[:, j] for j in range(heads_here)], axis=1).astype(
        jnp.bfloat16
    )

    def product(target):
        start = pl.multiple_of(target * out_cols, out_cols)
        part = jnp.dot(mine, wo[:, pl.ds(start, out_cols)], preferred_element_type=jnp.float32)
        return jnp.concatenate([part[:, b * HD : (b + 1) * HD] for b in range(blocks)], axis=0)

    def send_part(i, carry):
        k = n // 2 + (1 - 2 * (i % 2)) * ((i + 1) // 2)
        target = (me + k) % n
        parts_out[k - 1] = product(target).astype(jnp.bfloat16)
        pltpu.make_async_remote_copy(
            src_ref=parts_out.at[k - 1],
            dst_ref=parts_in.at[k - 1],
            send_sem=d_send,
            recv_sem=d_recv,
            device_id={"wx": target},
            device_id_type=pl.DeviceIdType.MESH,
        ).start()
        return carry

    lax.fori_loop(0, n - 1, send_part, 0)
    result = product(me)
    all_parts = pltpu.make_async_remote_copy(
        src_ref=parts_out,
        dst_ref=parts_in,
        send_sem=d_send,
        recv_sem=d_recv,
        device_id={"wx": (me + 1) % n},
        device_id_type=pl.DeviceIdType.MESH,
    )
    all_parts.wait_recv()
    for k in range(n - 1):
        result = result + parts_in[k].astype(jnp.float32)
    out_ref[...] = jnp.concatenate(
        [result[b * batch : (b + 1) * batch] for b in range(blocks)], axis=1
    ).astype(jnp.bfloat16)

    all_parts.wait_send()
    all_terms().wait_send()
    for i in range(sharers):
        target = my_head * sharers + i

        @pl.when(target != me)
        def _():
            attended_copy(i, my_row, target).wait_send()


def fused(n, hidden_in, norm_gain, w_query, w_key, w_value, w_out, key_cache, value_cache, lengths):
    batch, features = hidden_in.shape
    ctx = key_cache.shape[1]
    out_cols = w_out.shape[1] // n
    part_rows = batch * out_cols // HD
    q_chunks = w_query.shape[1] // QCOLS
    vmem = pl.BlockSpec(memory_space=pltpu.VMEM)
    hbm = pl.BlockSpec(memory_space=pl.ANY)
    smem = pl.BlockSpec(memory_space=pltpu.SMEM)
    bf16, f32 = jnp.bfloat16, jnp.float32
    return pl.pallas_call(
        functools.partial(fused_kernel, n, batch),
        out_shape=jax.ShapeDtypeStruct((batch, out_cols), bf16),
        in_specs=[vmem, vmem, smem] + [hbm] * 6,
        out_specs=vmem,
        scratch_shapes=[
            pltpu.VMEM((q_chunks, features, QCOLS), bf16),
            pltpu.VMEM((features, 2 * KVH * HD), bf16),
            pltpu.VMEM(w_out.shape, bf16),
            pltpu.VMEM((ctx, HD), bf16),
            pltpu.VMEM((ctx, HD), bf16),
            pltpu.VMEM((n * MSG, HD), f32),
            pltpu.VMEM((n - 1, MSG, HD), f32),
            pltpu.VMEM((G, ctx), f32),
            pltpu.VMEM((G * HD // w_out.shape[0], 8, HD), f32),
            pltpu.VMEM((batch, 8, HD), f32),
            pltpu.VMEM((n - 1, part_rows, HD), bf16),
            pltpu.VMEM((n - 1, part_rows, HD), bf16),
            pltpu.SemaphoreType.DMA((q_chunks,)),
            pltpu.SemaphoreType.DMA((2,)),
            pltpu.SemaphoreType.DMA((WO_PIECES,)),
            pltpu.SemaphoreType.DMA((2,)),
            pltpu.SemaphoreType.DMA,
            pltpu.SemaphoreType.DMA,
            pltpu.SemaphoreType.DMA((G * HD // w_out.shape[0],)),
            pltpu.SemaphoreType.DMA((batch,)),
            pltpu.SemaphoreType.DMA,
            pltpu.SemaphoreType.DMA,
        ],
        compiler_params=pltpu.CompilerParams(
            collective_id=0, has_side_effects=True, vmem_limit_bytes=56 * 1024 * 1024
        ),
    )(
        hidden_in, norm_gain, lengths, w_query, w_key, w_value, w_out,
        key_cache, value_cache,
    )


def choose(n, *arrays):
    hidden_in, w_out, key_cache = arrays[0], arrays[5], arrays[6]
    rows_here = w_out.shape[0]
    fits = (
        key_cache.shape[0] == 1
        and hidden_in.shape[0] * KVH == n
        and rows_here % HD == 0
        and (G * HD) % rows_here == 0
        and rows_here <= 8 * HD
        and rows_here % (16 * WO_PIECES) == 0
        and key_cache.shape[1] % SCORE_BLOCK == 0
        and (hidden_in.shape[0] * (w_out.shape[1] // n // HD)) % 16 == 0
    )
    return fused(n, *arrays) if fits else local(*arrays)


def solution(mesh):
    in_specs = (
        P("group", "wx"),
        P("wx"),
        P("wx", None),
        P("wx", None),
        P("wx", None),
        P("wx", None),
        P(("group", "wx"), None, None),
        P(("group", "wx"), None, None),
        P("group"),
    )
    out_specs = P("group", "wx")
    return jax.shard_map(
        functools.partial(choose, mesh.shape["wx"]), mesh=mesh, in_specs=in_specs, out_specs=out_specs, check_vma=False)
```
